32 devices in a mesh: grp: 2 (over y), wide: 8 (over z, x), sec: 2 (over core).
Axes of the slice: x: 2, y: 2, z: 4, core: 2. Of those that a mesh axis runs over, the one named last changes fastest.
Arguments:
- dosage: bfloat16 [4096, 16384], P(('sec', 'wide'), 'grp'), parts along dimension 1, may hold values from 0 to 2
- weights: bfloat16 [20, 24, 128, 128], P(None, 'sec'), may hold values from -0.109375 to 0.109375
- blocks: int32 [20, 24], P(None, 'sec'), may hold values from 0 to 15, as said below
- flips: int32 [4096], P('sec'), may hold values 0 or 1
Outputs:
- scores: float32 [16384, 2560], P(('grp', 'wide'), 'sec'), parts along dimension 0
The draws below stay inside these ranges and needn't reach their ends.
There are 2 independent parts, one for each index of `grp`. The reference program is written for one: setup_inputs(seed, part) draws one part's arguments, and reference() takes and returns one part's arrays. A program takes and returns all parts, laid end to end along the dimension named above; an argument that names none is the same for every part. Nothing has to cross between parts.
Inputs may be any that keep to these rules, and one draw needn't show every extreme that they name: blocks[t, k] counts within the section of variants k // 12; within one tile and one section the 12 block numbers are distinct.
All inputs are finite; a program needn't handle non-finite values. No bound on the sum of `flips` on one device may be relied on, other than what follows from the above.
Results may differ from the reference program's by a relative error of at most 0.0003.
Values may be sent and summed in bfloat16 or wider, within the bound.
A program may use at most 128 MiB of HBM per device.

```python
import jax
import jax.numpy as jnp
from jax import lax

BLOCK = 128
SCORES = 2560
VARIANTS = 4096
NNZ_SEC = 12
SAMPLES = 8192
TILES = 20
BLK_SEC = 16
NNZ = 24
N_SEC = 2


def draw_blocks(key, part):
    key = jax.random.fold_in(key, 5)
    count = TILES * N_SEC
    row_keys = jax.random.split(key, count)
    rows = jnp.arange(count, dtype=jnp.int32)

    def one_row(row_key, row):
        order = jax.random.permutation(row_key, BLK_SEC).astype(jnp.int32)
        chosen = order[:NNZ_SEC]
        top_shift = (chosen + BLK_SEC - 1 - chosen[0]) % BLK_SEC
        low_shift = (chosen + BLK_SEC - chosen[0]) % BLK_SEC
        chosen = jnp.where(row == 0, top_shift, chosen)
        chosen = jnp.where(row == 1, low_shift, chosen)
        return chosen.astype(jnp.int32)
    picked = jax.vmap(one_row)(row_keys, rows)
    return picked.reshape(TILES, N_SEC * NNZ_SEC).astype(jnp.int32)


def touch_ends(drawn, stream_key, least, top_value):
    extent = drawn.shape
    spot = [jax.random.randint(jax.random.fold_in(stream_key, axis), (), 0, extent[axis]) for axis in range(len(extent))]
    drawn = drawn.at[tuple(spot)].set(least)
    longest = extent.index(max(extent))
    spot[longest] = (spot[longest] + 1) % extent[longest]
    return drawn.at[tuple(spot)].set(top_value)


def level_of(stream_key, shape, cuts, least, top_value):
    level, own = 1.0, jax.random.fold_in(stream_key, 6)
    for dim, parts in cuts:
        draws = jnp.exp(jax.random.uniform(jax.random.fold_in(own, dim), (parts,), jnp.float32, least / len(cuts), top_value / len(cuts)))
        level = level * jnp.repeat(draws, shape[dim] // parts).reshape([-1 if axis == dim else 1 for axis in range(len(shape))])
    return level


def centred(rng, dims, width, most, cuts=(), kind=jnp.bfloat16):
    values = jax.random.normal(rng, dims, jnp.float32) * width
    if len(cuts) > 0:
        values = level_of(rng, dims, cuts, -0.22, 0.18) * values
    return jnp.clip(values, min=-most, max=most).astype(kind)


def setup_inputs(seed: int = 0, part: int = 0) -> dict:
    seeds = jax.random.split(jax.random.key(seed), 5)
    part_keys = jax.random.split(jax.random.fold_in(seeds[4], part), 5)
    return {
        "dosage": jnp.clip(2.0 * jax.random.uniform(part_keys[0], (VARIANTS, SAMPLES), jnp.float32) ** level_of(part_keys[0], (VARIANTS, SAMPLES), ((0, 16),), -0.2, 0.2), 0.0, 2.0).astype(jnp.bfloat16),
        "weights": centred(seeds[1], (TILES, NNZ, BLOCK, BLOCK), (NNZ * BLOCK) ** -0.5, 0.109375, ((1, 2),)),
        "blocks": draw_blocks(jax.random.fold_in(seeds[4], 71), part),
        "flips": touch_ends((jax.random.randint(seeds[3], (VARIANTS,), 0, 3) < 1).astype(jnp.int32), jax.random.fold_in(seeds[3], 1), 0, 1),
    }


def reference(dosage, weights, blocks, flips):
    first = (jnp.arange(NNZ, dtype=jnp.int32) // NNZ_SEC) * BLK_SEC
    global_blocks = (first[None, :] + blocks).astype(jnp.int32)
    flip_rows = flips.reshape(-1, BLOCK)[global_blocks]
    signed = jnp.where(flip_rows[..., None] == 1, -weights, weights)
    offset = 2.0 * jnp.einsum("tkr,tkrc->tc", flip_rows.astype(jnp.float32), weights.astype(jnp.float32))
    dosage_blocks = dosage.reshape(-1, BLOCK, dosage.shape[1])

    def one_tile(items):
        index_row, tile_weights, tile_offset = items
        picked = dosage_blocks[index_row].astype(jnp.float32)
        total = jnp.einsum("krs,krc->sc", picked, tile_weights.astype(jnp.float32))
        return total + tile_offset[None, :]

    tiles = lax.map(one_tile, (global_blocks, signed, offset))
    return jnp.transpose(tiles, (1, 0, 2)).reshape(dosage.shape[1], SCORES)
```

```python
import functools

import jax
import jax.numpy as jnp
from jax import lax
from jax.experimental import pallas as pl
from jax.experimental.pallas import tpu as pltpu
from jax.sharding import PartitionSpec as P

MESH = pl.DeviceIdType.MESH
MIB = 1024 * 1024


def partner_of(me, k):
    bit, out = 1, me
    while bit <= k:
        if k & bit:
            out = out + bit - 2 * bit * (lax.rem(lax.div(me, bit), 2))
        bit *= 2
    return out


def kernel(n, chunks, width, dos, wts, blocks, flips, out, x, dense, stage, raw_other, raw_own, sign, off, off_in, xt,
           send_sem, recv_sem, own_sem, fwd_send, fwd_recv, w_sem, d_send, d_recv, o_send, o_recv):
    me = lax.axis_index("wide")
    sec = lax.axis_index("sec")
    grp = lax.axis_index("grp")
    other = 1 - sec
    rows = dos.shape[0]
    samples = chunks * width
    tiles, nnz, block, _ = wts.shape
    half = tiles // 2
    count = flips.shape[0]
    power = n & (n - 1) == 0
    order = list(range(n - 1, 0, -1))
    peers = [partner_of(me, k) if power else lax.rem(me + k, n) for k in order]
    mine = pl.ds(pl.multiple_of(me * rows, rows), rows)

    barrier = pltpu.get_barrier_semaphore()
    for peer in peers:
        pl.semaphore_signal(barrier, inc=1, device_id=(grp, peer, sec), device_id_type=MESH)
    pl.semaphore_signal(barrier, inc=1, device_id=(grp, me, other), device_id_type=MESH)

    load = [
        pltpu.make_async_copy(wts.at[pl.ds(h * half, half)], raw, w_sem.at[i])
        for i, (h, raw) in enumerate(((other, raw_other), (sec, raw_own)))
    ]
    for copy in load:
        copy.start()
    own = [
        pltpu.make_async_copy(
            dos.at[:, pl.ds(pl.multiple_of(me * samples + c * width, width), width)], x.at[c, sec, mine], own_sem.at[c]
        )
        for c in range(chunks)
    ]
    pl.semaphore_wait(barrier, n)

    for c in range(chunks):
        for peer in peers:
            pltpu.make_async_remote_copy(
                src_ref=dos.at[:, pl.ds(pl.multiple_of(peer * samples + c * width, width), width)],
                dst_ref=x.at[c, sec, mine],
                send_sem=send_sem.at[c],
                recv_sem=recv_sem.at[c],
                device_id=(grp, peer, sec),
                device_id_type=MESH,
            ).start()
    for copy in own:
        copy.start()

    for b in range(count):
        row = flips[b : b + 1, :].astype(jnp.float32)
        sign[b] = 1.0 - 2.0 * jnp.transpose(jnp.broadcast_to(row, (block, block)))

    def build(h, raw, put):
        def one(j, _):
            t = h * half + j
            total = jnp.zeros((block, block), jnp.float32)
            for b in range(count):
                at = jnp.int32(0)
                there = jnp.int32(0)
                for k in range(nnz):
                    same = blocks[t, k] == b
                    at = jnp.where(same, jnp.int32(k), at)
                    there = jnp.where(same, jnp.int32(1), there)
                value = raw[j, at].astype(jnp.float32) * there.astype(jnp.float32)
                signs = sign[b]
                total = total + (1.0 - signs) * value
                put(b, j, (value * signs).astype(jnp.bfloat16))
            line = jnp.sum(total, axis=0, keepdims=True)
            off[h, j] = jnp.broadcast_to(line, (8, block))
            return 0

        lax.fori_loop(0, half, one, 0)

    def put_stage(b, j, value):
        stage[b * block : (b + 1) * block, pl.ds(pl.multiple_of(j * block, block), block)] = value

    def put_dense(b, j, value):
        dense[sec, b * block : (b + 1) * block, pl.ds(pl.multiple_of(j * block, block), block)] = value

    load[0].wait()
    build(other, raw_other, put_stage)
    send_dense = pltpu.make_async_remote_copy(
        src_ref=stage, dst_ref=dense.at[sec], send_sem=d_send, recv_sem=d_recv,
        device_id=(grp, me, other), device_id_type=MESH,
    )
    send_off = pltpu.make_async_remote_copy(
        src_ref=off.at[other], dst_ref=off_in, send_sem=o_send, recv_sem=o_recv,
        device_id=(grp, me, other), device_id_type=MESH,
    )
    send_dense.start()
    send_off.start()
    load[1].wait()
    build(sec, raw_own, put_dense)
    pltpu.make_async_copy(stage, dense.at[other], d_recv).wait()
    send_off.wait_recv()

    depth = count * block
    step = 2 * block
    columns = half * block
    wide_n = 2 * block if columns % (2 * block) == 0 else block

    def multiply(c, which, first):
        def turn(i, _):
            r = pl.ds(pl.multiple_of(i * step, step), step)
            xt[:, r] = jnp.transpose(x[c, which, r, :])
            return 0

        lax.fori_loop(0, depth // step, turn, 0)

        def column(i, _):
            at = pl.ds(pl.multiple_of(i * wide_n, wide_n), wide_n)
            value = jnp.dot(xt[...], dense[which, :, at], preferred_element_type=jnp.float32)
            here = slice(c * width, (c + 1) * width)
            if first:
                per = wide_n // block
                line = jnp.concatenate(
                    [(off[sec, i * per + q] + off_in[i * per + q])[0:1, :] for q in range(per)], axis=1
                )
                out[here, at] = value + line
            else:
                out[here, at] += value
            return 0

        lax.fori_loop(0, columns // wide_n, column, 0)

    for c in range(chunks):
        own[c].wait()
        from_peers = x.at[c, sec, pl.ds(0, (n - 1) * rows)]
        pltpu.make_async_copy(from_peers, from_peers, recv_sem.at[c]).wait()
        forward = pltpu.make_async_remote_copy(
            src_ref=x.at[c, sec], dst_ref=x.at[c, sec], send_sem=fwd_send.at[c], recv_sem=fwd_recv.at[c],
            device_id=(grp, me, other), device_id_type=MESH,
        )
        forward.start()
        multiply(c, sec, True)
        pltpu.make_async_copy(x.at[c, sec], x.at[c, other], fwd_recv.at[c]).wait()
        multiply(c, other, False)
        forward.wait_send()

    for c in range(chunks):
        to_peers = x.at[c, sec, pl.ds(0, (n - 1) * rows)]
        pltpu.make_async_copy(to_peers, to_peers, send_sem.at[c]).wait()
    send_dense.wait_send()
    send_off.wait_send()


def solution(mesh):
    n = mesh.shape["wide"]
    chunks = 4

    def body(dosage, weights, blocks, flips):
        tiles, nnz, block, _ = weights.shape
        half = tiles // 2
        rows, everyone = dosage.shape
        samples = everyone // n
        width = samples // chunks
        depth = flips.shape[0]
        count = depth // block
        columns = half * block
        any_space = pl.BlockSpec(memory_space=pl.ANY)
        vmem = pl.BlockSpec(memory_space=pltpu.VMEM)
        return pl.pallas_call(
            functools.partial(kernel, n, chunks, width),
            out_shape=pltpu.VMEM((samples, columns), jnp.float32),
            in_specs=[any_space, any_space, pl.BlockSpec(memory_space=pltpu.SMEM), vmem],
            out_specs=vmem,
            scratch_shapes=[
                pltpu.VMEM((chunks, 2, depth, width), jnp.bfloat16),
                pltpu.VMEM((2, depth, columns), jnp.bfloat16),
                pltpu.VMEM((depth, columns), jnp.bfloat16),
                pltpu.VMEM((half, nnz, block, block), jnp.bfloat16),
                pltpu.VMEM((half, nnz, block, block), jnp.bfloat16),
                pltpu.VMEM((count, block, block), jnp.float32),
                pltpu.VMEM((2, half, 8, block), jnp.float32),
                pltpu.VMEM((half, 8, block), jnp.float32),
                pltpu.VMEM((width, depth), jnp.bfloat16),
                pltpu.SemaphoreType.DMA((chunks,)),
                pltpu.SemaphoreType.DMA((chunks,)),
                pltpu.SemaphoreType.DMA((chunks,)),
                pltpu.SemaphoreType.DMA((chunks,)),
                pltpu.SemaphoreType.DMA((chunks,)),
                pltpu.SemaphoreType.DMA((2,)),
                pltpu.SemaphoreType.DMA,
                pltpu.SemaphoreType.DMA,
                pltpu.SemaphoreType.DMA,
                pltpu.SemaphoreType.DMA,
            ],
            compiler_params=pltpu.CompilerParams(
                collective_id=0, has_side_effects=True, vmem_limit_bytes=50 * MIB
            ),
        )(dosage, weights, blocks, flips.reshape(count, block))

    in_specs = (P(("sec", "wide"), "grp"), P(None, "sec", None, None), P(None, "sec"), P("sec"))
    out_specs = P(("grp", "wide"), "sec")
    return jax.shard_map(body, mesh=mesh, in_specs=in_specs, out_specs=out_specs, check_vma=False)
```

```python
import functools

import jax
import jax.numpy as jnp
from jax import lax
from jax.experimental import pallas as pl
from jax.experimental.pallas import tpu as pltpu
from jax.sharding import PartitionSpec as P

MESH = pl.DeviceIdType.MESH
MIB = 1024 * 1024


def partner_of(me, k):
    bit, out = 1, me
    while bit <= k:
        if k & bit:
            out = out + bit - 2 * bit * (lax.rem(lax.div(me, bit), 2))
        bit *= 2
    return out


SHARES = (2, 2, 2, 1, 1)


def split(samples, block):
    unit = samples // sum(SHARES)
    if samples % sum(SHARES) or unit % block:
        return (samples,)
    return tuple(share * unit for share in SHARES)


def kernel(n, widths, dos, wts, blocks, flips, out, dense, stage, raw_other, raw_own, sign, off, off_in,
           send_sem, recv_sem, own_sem, fwd_send, fwd_recv, w_sem, d_send, d_recv, o_send, o_recv, *x):
    me = lax.axis_index("wide")
    sec = lax.axis_index("sec")
    grp = lax.axis_index("grp")
    other = 1 - sec
    rows = dos.shape[0]
    samples = sum(widths)
    chunks = len(widths)
    first_of = [sum(widths[:c]) for c in range(chunks)]
    tiles, nnz, block, _ = wts.shape
    half = tiles // 2
    count = flips.shape[0]
    power = n & (n - 1) == 0
    order = list(range(1, n))
    peers = [partner_of(me, k) if power else lax.rem(me + k, n) for k in order]
    mine = pl.ds(pl.multiple_of(me * rows, rows), rows)

    barrier = pltpu.get_barrier_semaphore()
    for peer in peers:
        pl.semaphore_signal(barrier, inc=1, device_id=(grp, peer, sec), device_id_type=MESH)
    pl.semaphore_signal(barrier, inc=1, device_id=(grp, me, other), device_id_type=MESH)

    load = [
        pltpu.make_async_copy(wts.at[pl.ds(h * half, half)], raw, w_sem.at[i])
        for i, (h, raw) in enumerate(((other, raw_other), (sec, raw_own)))
    ]
    for copy in load:
        copy.start()
    own = [
        pltpu.make_async_copy(
            dos.at[:, pl.ds(pl.multiple_of(me * samples + first_of[c], block), widths[c])], x[c].at[sec, mine], own_sem.at[c]
        )
        for c in range(chunks)
    ]
    pl.semaphore_wait(barrier, n)

    for c in range(chunks):
        for peer in peers:
            pltpu.make_async_remote_copy(
                src_ref=dos.at[:, pl.ds(pl.multiple_of(peer * samples + first_of[c], block), widths[c])],
                dst_ref=x[c].at[sec, mine],
                send_sem=send_sem.at[c],
                recv_sem=recv_sem.at[c],
                device_id=(grp, peer, sec),
                device_id_type=MESH,
            ).start()
    for copy in own:
        copy.start()

    for b in range(count):
        row = flips[b : b + 1, :].astype(jnp.float32)
        sign[b] = 1.0 - 2.0 * jnp.transpose(jnp.broadcast_to(row, (block, block)))

    def build(h, raw, put):
        def one(j, _):
            t = h * half + j
            total = jnp.zeros((block, block), jnp.float32)
            for b in range(count):
                at = jnp.int32(0)
                there = jnp.int32(0)
                for k in range(nnz):
                    same = blocks[k, t] == b
                    at = jnp.where(same, jnp.int32(k), at)
                    there = jnp.where(same, jnp.int32(1), there)
                value = raw[j, at].astype(jnp.float32) * there.astype(jnp.float32)
                signs = sign[b]
                total = total + (1.0 - signs) * value
                put(b, j, (value * signs).astype(jnp.bfloat16))
            line = jnp.sum(total, axis=0, keepdims=True)
            off[h, j] = jnp.broadcast_to(line, (8, block))
            return 0

        lax.fori_loop(0, half, one, 0)

    def put_stage(b, j, value):
        stage[b * block : (b + 1) * block, pl.ds(pl.multiple_of(j * block, block), block)] = value

    def put_dense(b, j, value):
        dense[sec, b * block : (b + 1) * block, pl.ds(pl.multiple_of(j * block, block), block)] = value

    load[0].wait()
    build(other, raw_other, put_stage)
    send_dense = pltpu.make_async_remote_copy(
        src_ref=stage, dst_ref=dense.at[sec], send_sem=d_send, recv_sem=d_recv,
        device_id=(grp, me, other), device_id_type=MESH,
    )
    send_off = pltpu.make_async_remote_copy(
        src_ref=off.at[other], dst_ref=off_in, send_sem=o_send, recv_sem=o_recv,
        device_id=(grp, me, other), device_id_type=MESH,
    )
    send_dense.start()
    send_off.start()
    load[1].wait()
    build(sec, raw_own, put_dense)
    pltpu.make_async_copy(stage, dense.at[other], d_recv).wait()
    send_off.wait_recv()

    depth = count * block
    columns = half * block
    wide_n = 2 * block if columns % (2 * block) == 0 else block

    def multiply(c, which, first):
        width = widths[c]

        def column(i, _):
            at = pl.ds(pl.multiple_of(i * wide_n, wide_n), wide_n)
            value = lax.dot_general(x[c][which], dense[which, :, at], (((0,), (0,)), ((), ())), preferred_element_type=jnp.float32)
            here = slice(first_of[c], first_of[c] + width)
            if first:
                per = wide_n // block
                line = jnp.concatenate(
                    [(off[sec, i * per + q] + off_in[i * per + q])[0:1, :] for q in range(per)], axis=1
                )
                out[here, at] = value + line
            else:
                out[here, at] += value
            return 0

        lax.fori_loop(0, columns // wide_n, column, 0)

    for c in range(chunks):
        own[c].wait()
        from_peers = x[c].at[sec, pl.ds(0, (n - 1) * rows)]
        pltpu.make_async_copy(from_peers, from_peers, recv_sem.at[c]).wait()
        forward = pltpu.make_async_remote_copy(
            src_ref=x[c].at[sec], dst_ref=x[c].at[sec], send_sem=fwd_send.at[c], recv_sem=fwd_recv.at[c],
            device_id=(grp, me, other), device_id_type=MESH,
        )
        forward.start()
        multiply(c, sec, True)
        pltpu.make_async_copy(x[c].at[sec], x[c].at[other], fwd_recv.at[c]).wait()
        multiply(c, other, False)
        forward.wait_send()

    for c in range(chunks):
        to_peers = x[c].at[sec, pl.ds(0, (n - 1) * rows)]
        pltpu.make_async_copy(to_peers, to_peers, send_sem.at[c]).wait()
    send_dense.wait_send()
    send_off.wait_send()


def solution(mesh):
    n = mesh.shape["wide"]

    def body(dosage, weights, blocks, flips):
        tiles, nnz, block, _ = weights.shape
        half = tiles // 2
        rows, everyone = dosage.shape
        samples = everyone // n
        widths = split(samples, block)
        chunks = len(widths)
        depth = flips.shape[0]
        count = depth // block
        columns = half * block
        any_space = pl.BlockSpec(memory_space=pl.ANY)
        vmem = pl.BlockSpec(memory_space=pltpu.VMEM)
        return pl.pallas_call(
            functools.partial(kernel, n, widths),
            out_shape=pltpu.VMEM((samples, columns), jnp.float32),
            in_specs=[any_space, any_space, pl.BlockSpec(memory_space=pltpu.SMEM), vmem],
            out_specs=vmem,
            scratch_shapes=[
                pltpu.VMEM((2, depth, columns), jnp.bfloat16),
                pltpu.VMEM((depth, columns), jnp.bfloat16),
                pltpu.VMEM((half, nnz, block, block), jnp.bfloat16),
                pltpu.VMEM((half, nnz, block, block), jnp.bfloat16),
                pltpu.VMEM((count, block, block), jnp.float32),
                pltpu.VMEM((2, half, 8, block), jnp.float32),
                pltpu.VMEM((half, 8, block), jnp.float32),
                pltpu.SemaphoreType.DMA((chunks,)),
                pltpu.SemaphoreType.DMA((chunks,)),
                pltpu.SemaphoreType.DMA((chunks,)),
                pltpu.SemaphoreType.DMA((chunks,)),
                pltpu.SemaphoreType.DMA((chunks,)),
                pltpu.SemaphoreType.DMA((2,)),
                pltpu.SemaphoreType.DMA,
                pltpu.SemaphoreType.DMA,
                pltpu.SemaphoreType.DMA,
                pltpu.SemaphoreType.DMA,
                *[pltpu.VMEM((2, depth, width), jnp.bfloat16) for width in widths],
            ],
            compiler_params=pltpu.CompilerParams(
                collective_id=0, has_side_effects=True, vmem_limit_bytes=50 * MIB
            ),
        )(dosage, weights, blocks.T, flips.reshape(count, block))

    in_specs = (P(("sec", "wide"), "grp"), P(None, "sec", None, None), P(None, "sec"), P("sec"))
    out_specs = P(("grp", "wide"), "sec")
    return jax.shard_map(body, mesh=mesh, in_specs=in_specs, out_specs=out_specs, check_vma=False)
```

```python
import functools

import jax
import jax.numpy as jnp
from jax import lax
from jax.experimental import pallas as pl
from jax.experimental.pallas import tpu as pltpu
from jax.sharding import PartitionSpec as P

MESH = pl.DeviceIdType.MESH
MIB = 1024 * 1024


def partner_of(me, k):
    bit, out = 1, me
    while bit <= k:
        if k & bit:
            out = out + bit - 2 * bit * (lax.rem(lax.div(me, bit), 2))
        bit *= 2
    return out


SHARES = (2, 2, 2, 1, 1)


def split(samples, block):
    unit = samples // sum(SHARES)
    if samples % sum(SHARES) or unit % block:
        return (samples,)
    return tuple(share * unit for share in SHARES)


def kernel(n, widths, dos, wts, blocks, flips, out, dense, stage, raw_other, raw_own, sign, off, off_in,
           send_sem, recv_sem, own_sem, fwd_send, fwd_recv, w_sem, d_send, d_recv, o_send, o_recv, *x):
    me = lax.axis_index("wide")
    sec = lax.axis_index("sec")
    grp = lax.axis_index("grp")
    other = 1 - sec
    rows = dos.shape[0]
    samples = sum(widths)
    chunks = len(widths)
    first_of = [sum(widths[:c]) for c in range(chunks)]
    tiles, nnz, block, _ = wts.shape
    half = tiles // 2
    count = flips.shape[0]
    power = n & (n - 1) == 0
    order = list(range(1, n))
    peers = [partner_of(me, k) if power else lax.rem(me + k, n) for k in order]
    near = n // 2 - 1
    mine = pl.ds(pl.multiple_of(me * rows, rows), rows)

    barrier = pltpu.get_barrier_semaphore()
    for peer in peers:
        pl.semaphore_signal(barrier, inc=1, device_id=(grp, peer, sec), device_id_type=MESH)
    pl.semaphore_signal(barrier, inc=1, device_id=(grp, me, other), device_id_type=MESH)

    load = [
        pltpu.make_async_copy(wts.at[pl.ds(h * half, half)], raw, w_sem.at[i])
        for i, (h, raw) in enumerate(((other, raw_other), (sec, raw_own)))
    ]
    for copy in load:
        copy.start()
    own = [
        pltpu.make_async_copy(
            dos.at[:, pl.ds(pl.multiple_of(me * samples + first_of[c], block), widths[c])], x[c].at[sec, mine], own_sem.at[c]
        )
        for c in range(chunks)
    ]
    pl.semaphore_wait(barrier, n)

    for c in range(chunks):
        for i, peer in enumerate(peers):
            pltpu.make_async_remote_copy(
                src_ref=dos.at[:, pl.ds(pl.multiple_of(peer * samples + first_of[c], block), widths[c])],
                dst_ref=x[c].at[sec, mine],
                send_sem=send_sem.at[c],
                recv_sem=recv_sem.at[c, int(i >= near)],
                device_id=(grp, peer, sec),
                device_id_type=MESH,
            ).start()
    for copy in own:
        copy.start()

    for b in range(count):
        row = flips[b : b + 1, :].astype(jnp.float32)
        sign[b] = 1.0 - 2.0 * jnp.transpose(jnp.broadcast_to(row, (block, block)))

    def build(h, raw, put):
        def one(j, _):
            t = h * half + j
            total = jnp.zeros((block, block), jnp.float32)
            for b in range(count):
                at = jnp.int32(0)
                there = jnp.int32(0)
                for k in range(nnz):
                    same = blocks[k, t] == b
                    at = jnp.where(same, jnp.int32(k), at)
                    there = jnp.where(same, jnp.int32(1), there)
                value = raw[j, at].astype(jnp.float32) * there.astype(jnp.float32)
                signs = sign[b]
                total = total + (1.0 - signs) * value
                put(b, j, (value * signs).astype(jnp.bfloat16))
            line = jnp.sum(total, axis=0, keepdims=True)
            off[h, j] = jnp.broadcast_to(line, (8, block))
            return 0

        lax.fori_loop(0, half, one, 0)

    def put_stage(b, j, value):
        stage[b * block : (b + 1) * block, pl.ds(pl.multiple_of(j * block, block), block)] = value

    def put_dense(b, j, value):
        dense[sec, b * block : (b + 1) * block, pl.ds(pl.multiple_of(j * block, block), block)] = value

    load[0].wait()
    build(other, raw_other, put_stage)
    send_dense = pltpu.make_async_remote_copy(
        src_ref=stage, dst_ref=dense.at[sec], send_sem=d_send, recv_sem=d_recv,
        device_id=(grp, me, other), device_id_type=MESH,
    )
    send_off = pltpu.make_async_remote_copy(
        src_ref=off.at[other], dst_ref=off_in, send_sem=o_send, recv_sem=o_recv,
        device_id=(grp, me, other), device_id_type=MESH,
    )
    send_dense.start()
    send_off.start()
    load[1].wait()
    build(sec, raw_own, put_dense)
    pltpu.make_async_copy(stage, dense.at[other], d_recv).wait()
    send_off.wait_recv()

    depth = count * block
    columns = half * block
    wide_n = 2 * block if columns % (2 * block) == 0 else block

    def multiply(c, which, first):
        width = widths[c]

        def column(i, _):
            at = pl.ds(pl.multiple_of(i * wide_n, wide_n), wide_n)
            value = lax.dot_general(x[c][which], dense[which, :, at], (((0,), (0,)), ((), ())), preferred_element_type=jnp.float32)
            here = slice(first_of[c], first_of[c] + width)
            if first:
                per = wide_n // block
                line = jnp.concatenate(
                    [(off[sec, i * per + q] + off_in[i * per + q])[0:1, :] for q in range(per)], axis=1
                )
                out[here, at] = value + line
            else:
                out[here, at] += value
            return 0

        lax.fori_loop(0, columns // wide_n, column, 0)

    def forward(c, owner):
        there = x[c].at[sec, pl.ds(pl.multiple_of(owner * rows, rows), rows)]
        pltpu.make_async_remote_copy(
            src_ref=there, dst_ref=there, send_sem=fwd_send.at[c], recv_sem=fwd_recv.at[c],
            device_id=(grp, me, other), device_id_type=MESH,
        ).start()

    for c in range(chunks):
        own[c].wait()
        forward(c, me)
        for g, group in enumerate((peers[:near], peers[near:])):
            if group:
                landed = x[c].at[sec, pl.ds(0, len(group) * rows)]
                pltpu.make_async_copy(landed, landed, recv_sem.at[c, g]).wait()
            for peer in group:
                forward(c, peer)
        multiply(c, sec, True)
        pltpu.make_async_copy(x[c].at[sec], x[c].at[other], fwd_recv.at[c]).wait()
        multiply(c, other, False)
        pltpu.make_async_copy(x[c].at[sec], x[c].at[sec], fwd_send.at[c]).wait()

    for c in range(chunks):
        to_peers = x[c].at[sec, pl.ds(0, (n - 1) * rows)]
        pltpu.make_async_copy(to_peers, to_peers, send_sem.at[c]).wait()
    send_dense.wait_send()
    send_off.wait_send()


def solution(mesh):
    n = mesh.shape["wide"]

    def body(dosage, weights, blocks, flips):
        tiles, nnz, block, _ = weights.shape
        half = tiles // 2
        rows, everyone = dosage.shape
        samples = everyone // n
        widths = split(samples, block)
        chunks = len(widths)
        depth = flips.shape[0]
        count = depth // block
        columns = half * block
        any_space = pl.BlockSpec(memory_space=pl.ANY)
        vmem = pl.BlockSpec(memory_space=pltpu.VMEM)
        return pl.pallas_call(
            functools.partial(kernel, n, widths),
            out_shape=pltpu.VMEM((samples, columns), jnp.float32),
            in_specs=[any_space, any_space, pl.BlockSpec(memory_space=pltpu.SMEM), vmem],
            out_specs=vmem,
            scratch_shapes=[
                pltpu.VMEM((2, depth, columns), jnp.bfloat16),
                pltpu.VMEM((depth, columns), jnp.bfloat16),
                pltpu.VMEM((half, nnz, block, block), jnp.bfloat16),
                pltpu.VMEM((half, nnz, block, block), jnp.bfloat16),
                pltpu.VMEM((count, block, block), jnp.float32),
                pltpu.VMEM((2, half, 8, block), jnp.float32),
                pltpu.VMEM((half, 8, block), jnp.float32),
                pltpu.SemaphoreType.DMA((chunks,)),
                pltpu.SemaphoreType.DMA((chunks, 2)),
                pltpu.SemaphoreType.DMA((chunks,)),
                pltpu.SemaphoreType.DMA((chunks,)),
                pltpu.SemaphoreType.DMA((chunks,)),
                pltpu.SemaphoreType.DMA((2,)),
                pltpu.SemaphoreType.DMA,
                pltpu.SemaphoreType.DMA,
                pltpu.SemaphoreType.DMA,
                pltpu.SemaphoreType.DMA,
                *[pltpu.VMEM((2, depth, width), jnp.bfloat16) for width in widths],
            ],
            compiler_params=pltpu.CompilerParams(
                collective_id=0, has_side_effects=True, vmem_limit_bytes=50 * MIB
            ),
        )(dosage, weights, blocks.T, flips.reshape(count, block))

    in_specs = (P(("sec", "wide"), "grp"), P(None, "sec", None, None), P(None, "sec"), P("sec"))
    out_specs = P(("grp", "wide"), "sec")
    return jax.shard_map(body, mesh=mesh, in_specs=in_specs, out_specs=out_specs, check_vma=False)
```
